32 devices in a mesh: rep: 4 (over y, core), fsdp: 8 (over z, x).
Axes of the slice: x: 2, y: 2, z: 4, core: 2. Of those that a mesh axis runs over, the one named last changes fastest.
Arguments:
- acts: bfloat16 [16384, 8192], P(('rep', 'fsdp')), may hold values from -12 to 12
- tok_grads: bfloat16 [16384, 1024], P(('rep', 'fsdp')), may hold values from -64 to 64
- log_ratio: float32 [16384], P(('rep', 'fsdp')), may hold values from -3 to 3
- loss_mask: int32 [16384], P(('rep', 'fsdp')), may hold values 0 or 1
- pairs: int32 [4, 8], P('rep'), may hold values from 0 to 7, each once within a row
- inner_w: float32 [4, 8192, 1024], P('rep', 'fsdp'), may hold values from -6 to 6
- adam_m: float32 [4, 8192, 1024], P('rep', 'fsdp'), may hold values from -3 to 3
- adam_v: float32 [4, 8192, 1024], P('rep', 'fsdp'), may hold values from 0.05 to 1
- anchor: float32 [8192, 1024], P('fsdp'), may hold values from -6 to 6
- outer_mom: float32 [8192, 1024], P('fsdp'), may hold values from -1.75 to 1.75
Outputs:
- input_grad: bfloat16 [16384, 8192], P(('rep', 'fsdp'))
- new_anchor: float32 [8192, 1024], P('fsdp')
- new_mom: float32 [8192, 1024], P('fsdp')
- new_m: float32 [4, 8192, 1024], P('rep', 'fsdp')
The draws below stay inside these ranges and needn't reach their ends.
Inputs may be any that keep to these rules, and one draw needn't show every extreme that they name: Each row of pairs is a permutation of 0 to 7; chosen sequence c of a group pairs with rejected sequence 8 + pairs[r, c].
All inputs are finite; a program needn't handle non-finite values. No bound on the sum of `loss_mask` on one device may be relied on, other than what follows from the above.
Results may differ from the reference program's by a relative error of at most 0.0057.
Values may be sent and summed in bfloat16 or wider, within the bound.
A program may use at most 128 MiB of HBM per device.

```python
import math
import jax
import jax.numpy as jnp
from jax import lax

D = 8192
KVW = 1024
SEQLEN = 256
SEQ_DEV = 2
HALF = 8
TOKENS = 16384
N_REP = 4
N_FSDP = 8


def plant(drawn, key, smallest, top_value):
    spot = [jax.random.randint(jax.random.fold_in(key, axis), (), 0, length) for axis, length in enumerate(drawn.shape)]
    main_axis = drawn.shape.index(max(drawn.shape))
    beside = spot[:main_axis] + [(spot[main_axis] + 1) % drawn.shape[main_axis]] + spot[main_axis + 1:]
    return drawn.at[tuple(spot)].set(smallest).at[tuple(beside)].set(top_value)


def with_spikes(array, key, source, target, blocks, factor):
    owner, partner = [(jnp.arange(array.shape[dim]) // (array.shape[dim] // blocks)).reshape([-1 if axis == dim else 1 for axis in range(array.ndim)]) for dim in (source, target)]
    chosen = jax.random.permutation(key, blocks)[partner]
    strong = (owner == chosen) | (owner == (partner + blocks // 2) % blocks)
    return jnp.where(strong, factor * array, array)


def block_scale(key, extent, cuts, smallest, top_value):
    gain = 1.0
    for axis_at, blocks in cuts:
        steps = jax.random.uniform(jax.random.fold_in(jax.random.fold_in(key, 6), axis_at), (blocks,), jnp.float32, smallest / len(cuts), top_value / len(cuts))
        gain = gain * jnp.repeat(jnp.exp(steps), extent[axis_at] // blocks).reshape((-1,) + (1,) * (len(extent) - 1 - axis_at))
    return gain


def normal_values(rng, dims, spread, limit, pieces=(), held_as=jnp.bfloat16):
    loudness = block_scale(rng, dims, pieces, -0.22, 0.18) if pieces else 1.0
    drawn = jax.random.normal(rng, dims, jnp.float32) * spread * loudness
    return jnp.minimum(jnp.maximum(drawn, -limit), limit).astype(held_as)


def heavy_noise(own_key, extent, deviation, bound, pieces, heavy, kind=jnp.bfloat16):
    drawn = deviation * jax.random.normal(own_key, extent, jnp.float32)
    if pieces:
        drawn = drawn * block_scale(own_key, extent, pieces, -0.22, 0.18)
    return jnp.clip(with_spikes(drawn, jax.random.fold_in(own_key, 3), *heavy), -bound, bound).astype(kind)


def setup_inputs(seed: int = 0) -> dict:
    splits = jax.random.split(jax.random.key(seed), 11)
    return {
        "acts": heavy_noise(splits[0], (TOKENS, D), 1.0, 12.0, ((0, 32),), (0, 1, 32, 2.75)),
        "tok_grads": normal_values(splits[1], (TOKENS, KVW), 10.0, 64.0, ((0, 32),)),
        "log_ratio": normal_values(splits[2], (TOKENS,), 0.5, 3.0, ((0, 32),), jnp.float32),
        "loss_mask": plant((jax.random.randint(splits[3], (TOKENS,), 0, 4) < 3).astype(jnp.int32), jax.random.fold_in(splits[3], 1), 0, 1),
        "pairs": jax.vmap(lambda own: jax.random.permutation(own, HALF))(jax.random.split(splits[4], N_REP)).reshape((N_REP, HALF)).astype(jnp.int32),
        "inner_w": normal_values(splits[5], (N_REP, D, KVW), 1.0, 6.0, ((0, 4), (1, 8)), jnp.float32),
        "adam_m": normal_values(splits[6], (N_REP, D, KVW), 0.5, 3.0, ((0, 4), (1, 8)), jnp.float32),
        "adam_v": jnp.clip(jnp.exp(math.log(1.0) - 2.9957323 * jax.random.uniform(splits[7], (N_REP, D, KVW), jnp.float32) ** block_scale(splits[7], (N_REP, D, KVW), ((0, 4), (1, 8)), -0.2, 0.2)), 0.05, 1.0),
        "anchor": normal_values(splits[8], (D, KVW), 1.0, 6.0, ((0, 8),), jnp.float32),
        "outer_mom": normal_values(splits[9], (D, KVW), 0.3, 1.75, ((0, 8),), jnp.float32),
    }


dpo_beta = 0.1
decay_one = 0.9
decay_two = 0.95
inner_rate = 0.05
weight_decay = 0.1
epsilon = 1e-08
momentum = 0.9
outer_rate = 0.7

def sequence_weights(ratios, mask_f, partner):
    seq_sums = (ratios * mask_f).reshape(-1, SEQLEN).sum(axis=1)
    half_n = partner.shape[0]
    onehot = (partner[:, None] == jnp.arange(half_n, dtype=jnp.int32)[None, :]).astype(jnp.float32)
    rejected = jnp.dot(onehot, seq_sums[half_n:], precision=lax.Precision.HIGHEST)
    margin = dpo_beta * (seq_sums[:half_n] - rejected)
    pull = jax.nn.sigmoid(-margin)
    push = jnp.dot(pull, onehot, precision=lax.Precision.HIGHEST)
    return jnp.concatenate([-dpo_beta * pull, dpo_beta * push])

def reference(acts, tok_grads, log_ratio, loss_mask, pairs, inner_w, adam_m, adam_v, anchor, outer_mom):
    scale = D ** (-0.5)
    rows = SEQ_DEV * SEQLEN
    group_tok = rows * N_FSDP
    grads_in = []
    moments = []
    delta_total = jnp.zeros((D, KVW), jnp.float32)
    for group in range(N_REP):
        lower = group * group_tok
        upper = lower + group_tok
        x_group = acts[lower:upper]
        mask_f = loss_mask[lower:upper].astype(jnp.float32)
        seq_weight = sequence_weights(log_ratio[lower:upper], mask_f, pairs[group])
        tok_weight = jnp.repeat(seq_weight, SEQLEN) * mask_f
        cot = (tok_weight[:, None] * tok_grads[lower:upper].astype(jnp.float32)).astype(jnp.bfloat16)
        w_half = inner_w[group].astype(jnp.bfloat16)
        grads_in.append((jnp.dot(cot, w_half.T, preferred_element_type=jnp.float32) * scale).astype(jnp.bfloat16))

        def add_block(running, blocks):
            x_block, cot_block = blocks
            term = lax.dot_general(x_block, cot_block, (((0,), (0,)), ((), ())), preferred_element_type=jnp.float32) * scale
            term = lax.optimization_barrier(term.astype(jnp.bfloat16))
            return (running + term.astype(jnp.float32), None)
        grad, _ = lax.scan(add_block, jnp.zeros((D, KVW), jnp.float32), (x_group.reshape(N_FSDP, rows, D), cot.reshape(N_FSDP, rows, KVW)))
        m_next = decay_one * adam_m[group] + (1.0 - decay_one) * grad
        v_next = decay_two * adam_v[group] + (1.0 - decay_two) * grad * grad
        inner_next = inner_w[group] - inner_rate * (m_next / (jnp.sqrt(v_next) + epsilon) + weight_decay * inner_w[group])
        moments.append(m_next)
        delta_total = delta_total + (anchor - inner_next)
    delta_avg = delta_total / N_REP
    new_mom = momentum * outer_mom + delta_avg
    new_anchor = anchor - outer_rate * (delta_avg + momentum * new_mom)
    return (jnp.concatenate(grads_in, axis=0), new_anchor, new_mom, jnp.stack(moments))
```

```python
import functools

import jax
import jax.numpy as jnp
from jax import lax
from jax.experimental import pallas as pl
from jax.experimental.pallas import tpu as pltpu
from jax.sharding import PartitionSpec as P

SEQLEN = 256

dpo_beta = 0.1
decay_one = 0.9
decay_two = 0.95
inner_rate = 0.05
weight_decay = 0.1
epsilon = 1e-08
momentum = 0.9
outer_rate = 0.7

MESH = pl.DeviceIdType.MESH


def pair_signs(partner, half_n):
    cols = jnp.arange(2 * half_n, dtype=jnp.int32)[None, :]
    chosen = jnp.arange(half_n, dtype=jnp.int32)[:, None]
    of_pair = (cols == chosen).astype(jnp.float32) - (cols == half_n + partner[:, None]).astype(jnp.float32)
    onehot = (partner[:, None] == jnp.arange(half_n, dtype=jnp.int32)[None, :]).astype(jnp.float32)
    of_rejected = jnp.sum(onehot[:, :, None] * of_pair[:, None, :], axis=0)
    return jnp.concatenate([of_pair, of_rejected])


def exchange_kernel(
    size, scale, acts, grads, w_own, sums, signs, input_grad, grad,
    all_sums, act, cot, w_all, up, down, stage,
    sums_tx, sums_rx, g_sem, local_sem, act_local, act_tx, act_rx, z_tx, z_rx, ig_local, ig_tx, ig_rx,
):
    n = size // 2
    me = lax.axis_index("fsdp")
    z, x = lax.div(me, 2), lax.rem(me, 2)
    peer = z * 2 + (1 - x)
    above, below = lax.rem(me + 2, size), lax.rem(me + size - 2, size)
    rows = acts.shape[0]
    feats, width = w_own.shape
    part = min(256, feats)
    parts = feats // part
    seqs = rows // SEQLEN

    def remote(src, dst, tx, rx, target):
        return pltpu.make_async_remote_copy(
            src_ref=src, dst_ref=dst, send_sem=tx, recv_sem=rx,
            device_id={"fsdp": target}, device_id_type=MESH,
        )

    def columns(block):
        return pl.ds(pl.multiple_of(block * feats, feats), feats)

    def load_acts(j):
        return pltpu.make_async_copy(
            acts.at[:, columns(j * 2 + x)], act.at[j, pl.ds(0, rows)], act_local.at[j])

    def send_block(j):
        return remote(
            acts.at[:, columns(j * 2 + 1 - x)], act.at[j, pl.ds(rows, rows)], act_tx.at[j], act_rx.at[j], peer)

    def send_acts(d):
        @pl.when(z + d <= n - 1)
        def _():
            send_block(z + d).start()

        @pl.when(jnp.logical_and(d > 0, z - d >= 0))
        def _():
            send_block(z - d).start()

    def w_copy(way, j, t_send, t_recv, target):
        return remote(w_all.at[j], w_all.at[j], z_tx.at[way, t_send], z_rx.at[way, t_recv], target)

    def sum_copy(way, j, t_send, t_recv, target):
        buf = up if way == 0 else down
        return remote(buf.at[j], buf.at[j], z_tx.at[way, t_send], z_rx.at[way, t_recv], target)

    own_w = pltpu.make_async_copy(w_own, w_all.at[z], local_sem.at[0])
    own_g = pltpu.make_async_copy(grads, cot.at[pl.ds(0, rows)], local_sem.at[1])
    own_w.start()
    own_g.start()

    @pl.loop(0, n)
    def _(j):
        load_acts(j).start()

    all_sums[me] = sums[...]

    barrier = pltpu.get_barrier_semaphore()

    @pl.loop(1, size)
    def _(k):
        pl.semaphore_signal(
            barrier, inc=1, device_id={"fsdp": lax.rem(me + k, size)}, device_id_type=MESH)

    pl.semaphore_wait(barrier, size - 1)

    @pl.loop(1, size)
    def _(k):
        remote(sums, all_sums.at[me], sums_tx.at[k], sums_rx.at[me], lax.rem(me + k, size)).start()

    peer_g = remote(grads, cot.at[pl.ds(rows, rows)], g_sem.at[0], g_sem.at[1], peer)
    peer_g.start()
    own_w.wait()

    @pl.when(z < n - 1)
    def _():
        w_copy(0, z, 0, 0, above).start()

    @pl.when(z > 0)
    def _():
        w_copy(1, z, 0, 0, below).start()

    send_acts(n - 1)

    @pl.loop(1, size)
    def _(k):
        source = lax.rem(me + k, size)
        remote(sums, all_sums.at[source], sums_tx.at[k], sums_rx.at[source], peer).wait_recv()

    own_g.wait()
    peer_g.wait_recv()
    if n >= 2:
        send_acts(n - 2)
    half_n = size * seqs // 2
    for q in range(2 * seqs):
        owner = me if q < seqs else peer
        seq = owner * seqs + q % seqs
        margin = dpo_beta * jnp.sum(jnp.sum(all_sums[...] * signs[q], axis=0), axis=0, keepdims=True)
        pull = 1.0 / (1.0 + jnp.exp(margin))
        weight = jnp.where(seq < half_n, -dpo_beta, dpo_beta) * pull
        span = pl.ds(q * SEQLEN, SEQLEN)
        for lane in range(0, width, 128):
            cell = cot[span, lane:lane + 128].astype(jnp.float32)
            cot[span, lane:lane + 128] = (weight * cell).astype(jnp.bfloat16)

    def partial(j):
        load_acts(j).wait()
        send_block(j).wait_recv()

        @pl.loop(0, parts)
        def _(c):
            span = pl.ds(pl.multiple_of(c * part, part), part)
            grad[span, :] = scale * lax.dot_general(
                act[j, :, span], cot[...], (((0,), (0,)), ((), ())), preferred_element_type=jnp.float32)

    def add_in(buf, j):
        @pl.loop(0, parts)
        def _(c):
            span = pl.ds(pl.multiple_of(c * part, part), part)
            grad[span, :] = grad[span, :] + buf[j, span, :].astype(jnp.float32)

    def pass_on(way, j, t):
        buf = up if way == 0 else down
        has_source = z > 0 if way == 0 else z < n - 1
        partial(j)

        @pl.when(has_source)
        def _():
            sum_copy(way, j, t, t - 1, peer).wait_recv()

            @pl.loop(0, parts)
            def _(c):
                span = pl.ds(pl.multiple_of(c * part, part), part)
                buf[j, span, :] = (grad[span, :] + buf[j, span, :].astype(jnp.float32)).astype(jnp.bfloat16)

        @pl.when(jnp.logical_not(has_source))
        def _():
            @pl.loop(0, parts)
            def _(c):
                span = pl.ds(pl.multiple_of(c * part, part), part)
                buf[j, span, :] = grad[span, :].astype(jnp.bfloat16)

        sum_copy(way, j, t, t, above if way == 0 else below).start()

    def ig_keep(j):
        return pltpu.make_async_copy(
            stage.at[j, pl.ds(0, rows)], input_grad.at[:, columns(j * 2 + x)], ig_local.at[j])

    def ig_send(j):
        return remote(
            stage.at[j, pl.ds(rows, rows)], input_grad.at[:, columns(j * 2 + x)], ig_tx.at[j], ig_rx.at[j], peer)

    def ig_arrival(j):
        return remote(
            stage.at[j, pl.ds(rows, rows)], input_grad.at[:, columns(j * 2 + 1 - x)], ig_tx.at[j], ig_rx.at[j], peer)

    def ig_block(j):
        @pl.loop(0, parts)
        def _(c):
            span = pl.ds(pl.multiple_of(c * part, part), part)
            stage[j, :, span] = (scale * lax.dot_general(
                cot[...], w_all[j, span, :], (((1,), (1,)), ((), ())), preferred_element_type=jnp.float32
            )).astype(jnp.bfloat16)

        ig_keep(j).start()
        ig_send(j).start()

    def slot(t, carry):
        d = n - t

        @pl.when(z >= t)
        def _():
            w_copy(0, z - t, t, t - 1, peer).wait_recv()

            @pl.when(z < n - 1)
            def _():
                w_copy(0, z - t, t, t, above).start()

        @pl.when(z + t <= n - 1)
        def _():
            w_copy(1, z + t, t, t - 1, peer).wait_recv()

            @pl.when(z > 0)
            def _():
                w_copy(1, z + t, t, t, below).start()

        @pl.when(z + d <= n - 1)
        def _():
            pass_on(0, z + d, t)

        @pl.when(z - d >= 0)
        def _():
            pass_on(1, z - d, t)

        @pl.when(d >= 2)
        def _():
            send_acts(d - 2)

        @pl.when(t == 1)
        def _():
            ig_block(z)

        @pl.when(z >= t)
        def _():
            ig_block(z - t)

        @pl.when(z + t <= n - 1)
        def _():
            ig_block(z + t)

        return carry

    lax.fori_loop(1, n, slot, 0)

    partial(z)

    @pl.when(z > 0)
    def _():
        sum_copy(0, z, n - 1, n - 1, peer).wait_recv()
        add_in(up, z)

    @pl.when(z < n - 1)
    def _():
        sum_copy(1, z, n - 1, n - 1, peer).wait_recv()
        add_in(down, z)

    @pl.loop(1, size)
    def _(k):
        remote(sums, all_sums.at[me], sums_tx.at[k], sums_rx.at[me], peer).wait_send()

    peer_g.wait_send()

    @pl.loop(0, n)
    def _(j):
        send_block(j).wait_send()
        w_way = j

        @pl.when(z < n - 1)
        def _():
            sum_copy(0, w_way, j, j, peer).wait_send()

        @pl.when(z > 0)
        def _():
            sum_copy(1, w_way, j, j, peer).wait_send()

        ig_keep(j).wait()
        ig_send(j).wait_send()
        ig_arrival(j).wait_recv()


def exchange(size, scale, acts, grads, w_half, sums, signs):
    n = size // 2
    rows, model = acts.shape
    feats, width = w_half.shape
    dma = pltpu.SemaphoreType.DMA
    bf16 = jnp.bfloat16
    anywhere = pl.BlockSpec(memory_space=pl.ANY)
    vmem = pl.BlockSpec(memory_space=pltpu.VMEM)
    return pl.pallas_call(
        functools.partial(exchange_kernel, size, scale),
        out_shape=(
            jax.ShapeDtypeStruct((rows, model), bf16),
            jax.ShapeDtypeStruct((feats, width), jnp.float32),
        ),
        in_specs=[anywhere, anywhere, anywhere, vmem, vmem],
        out_specs=(anywhere, vmem),
        scratch_shapes=[
            pltpu.VMEM((size,) + sums.shape, jnp.float32),
            pltpu.VMEM((n, 2 * rows, feats), bf16),
            pltpu.VMEM((2 * rows, width), bf16),
            pltpu.VMEM((n, feats, width), bf16),
            pltpu.VMEM((n, feats, width), bf16),
            pltpu.VMEM((n, feats, width), bf16),
            pltpu.VMEM((n, 2 * rows, feats), bf16),
            dma((size,)), dma((size,)), dma((2,)), dma((2,)),
            dma((n,)), dma((n,)), dma((n,)),
            dma((2, n)), dma((2, n)),
            dma((n,)), dma((n,)), dma((n,)),
        ],
        compiler_params=pltpu.CompilerParams(
            collective_id=0, has_side_effects=True, vmem_limit_bytes=60 * 1024 * 1024),
        cost_estimate=pl.CostEstimate(
            flops=8 * rows * model * width, bytes_accessed=6 * rows * model, transcendentals=0),
    )(acts, grads, w_half, sums, signs)


def outer_step(delta_avg, anchor_rows, mom_rows):
    mom_next = momentum * mom_rows + delta_avg
    anchor_next = anchor_rows - outer_rate * (delta_avg + momentum * mom_next)
    return (anchor_next, mom_next)


def local(acts, tok_grads, log_ratio, loss_mask, pairs, inner_w, adam_m, adam_v, anchor, outer_mom):
    size = lax.axis_size("fsdp")
    rows, model = acts.shape
    seqs = rows // SEQLEN
    scale = model ** (-0.5)
    mask_f = loss_mask.astype(jnp.float32)
    own_sums = (log_ratio * mask_f).reshape(seqs, SEQLEN).sum(axis=1)
    tile = -(-seqs // 8) * 8
    sums = jnp.zeros((tile, 128), jnp.float32).at[:seqs].set(jnp.broadcast_to(own_sums[:, None], (seqs, 128)))
    me = lax.axis_index("fsdp")
    peer = me + 1 - 2 * lax.rem(me, 2)
    table = pair_signs(pairs[0], size * seqs // 2)
    ours = jnp.concatenate([
        lax.dynamic_slice_in_dim(table, me * seqs, seqs),
        lax.dynamic_slice_in_dim(table, peer * seqs, seqs),
    ]).reshape(2 * seqs, size, seqs)
    signs = jnp.broadcast_to(
        jnp.pad(ours, ((0, 0), (0, 0), (0, tile - seqs)))[..., None], (2 * seqs, size, tile, 128))
    grads = jnp.where(loss_mask[:, None] != 0, tok_grads, jnp.zeros_like(tok_grads))
    w_half = inner_w[0].astype(jnp.bfloat16)
    input_grad, grad = exchange(size, scale, acts, grads, w_half, sums, signs)
    m_next = decay_one * adam_m[0] + (1.0 - decay_one) * grad
    v_next = decay_two * adam_v[0] + (1.0 - decay_two) * grad * grad
    inner_next = inner_w[0] - inner_rate * (
        m_next / (jnp.sqrt(v_next) + epsilon) + weight_decay * inner_w[0]
    )
    delta = anchor - inner_next
    groups = lax.axis_size("rep")
    delta_avg = lax.psum(delta, "rep") / groups
    new_anchor, new_mom = outer_step(delta_avg, anchor, outer_mom)
    return (input_grad, new_anchor, new_mom, m_next[None])


def solution(mesh):
    return jax.shard_map(
        local,
        mesh=mesh,
        in_specs=(
            P(("rep", "fsdp"), None),
            P(("rep", "fsdp"), None),
            P(("rep", "fsdp")),
            P(("rep", "fsdp")),
            P("rep", None),
            P("rep", "fsdp", None),
            P("rep", "fsdp", None),
            P("rep", "fsdp", None),
            P("fsdp", None),
            P("fsdp", None),
        ),
        out_specs=(
            P(("rep", "fsdp"), None),
            P("fsdp", None),
            P("fsdp", None),
            P("rep", "fsdp", None),
        ),
        check_vma=False,
    )
```

```python
import functools

import jax
import jax.numpy as jnp
from jax import lax
from jax.experimental import pallas as pl
from jax.experimental.pallas import tpu as pltpu
from jax.sharding import PartitionSpec as P

SEQLEN = 256

dpo_beta = 0.1
decay_one = 0.9
decay_two = 0.95
inner_rate = 0.05
weight_decay = 0.1
epsilon = 1e-08
momentum = 0.9
outer_rate = 0.7

CHUNKS = 8

MESH = pl.DeviceIdType.MESH


def pair_signs(partner, half_n):
    cols = jnp.arange(2 * half_n, dtype=jnp.int32)[None, :]
    chosen = jnp.arange(half_n, dtype=jnp.int32)[:, None]
    of_pair = (cols == chosen).astype(jnp.float32) - (cols == half_n + partner[:, None]).astype(jnp.float32)
    onehot = (partner[:, None] == jnp.arange(half_n, dtype=jnp.int32)[None, :]).astype(jnp.float32)
    of_rejected = jnp.sum(onehot[:, :, None] * of_pair[:, None, :], axis=0)
    return jnp.concatenate([of_pair, of_rejected])


def exchange_kernel(
    size, groups, scale, acts, grads, w_own, sums, signs, inner_w, adam_m, adam_v, anchor,
    input_grad, grad, delta_sum,
    all_sums, act, cot, w_all, running, stage, state, delta, core_in, y_parts,
    sums_tx, sums_rx, g_sem, local_sem, act_local, act_tx, act_rx, z_tx, z_rx, ig_local, ig_tx, ig_rx,
    state_sem, core_tx, core_rx, y_tx, y_rx, back_tx, back_rx,
):
    n = size // 2
    me = lax.axis_index("fsdp")
    z, x = lax.div(me, 2), lax.rem(me, 2)
    peer = z * 2 + (1 - x)
    above, below = lax.rem(me + 2, size), lax.rem(me + size - 2, size)
    rows = acts.shape[0]
    feats, width = w_own.shape
    part = min(256, feats)
    parts = feats // part
    seqs = rows // SEQLEN
    chunk = feats // CHUNKS
    half = chunk // 2
    pairs_y = groups // 2
    group = lax.axis_index("rep")
    y, core = lax.div(group, 2), lax.rem(group, 2)
    core_peer = y * 2 + (1 - core)

    def remote(src, dst, tx, rx, target, axis="fsdp"):
        return pltpu.make_async_remote_copy(
            src_ref=src, dst_ref=dst, send_sem=tx, recv_sem=rx,
            device_id={axis: target}, device_id_type=MESH,
        )

    def y_peer(k):
        return lax.rem(y + k, pairs_y) * 2 + core

    def chunk_rows(c):
        return pl.ds(pl.multiple_of(c * chunk, chunk), chunk)

    def half_rows(c, which):
        return pl.ds(pl.multiple_of(c * chunk + which * half, half), half)

    def packed_rows(c):
        return pl.ds(pl.multiple_of(c * half, half), half)

    def columns(block):
        return pl.ds(pl.multiple_of(block * feats, feats), feats)

    def load_acts(j):
        return pltpu.make_async_copy(
            acts.at[:, columns(j * 2 + x)], act.at[j, pl.ds(0, rows)], act_local.at[j])

    def send_block(j):
        return remote(
            acts.at[:, columns(j * 2 + 1 - x)], act.at[j, pl.ds(rows, rows)], act_tx.at[j], act_rx.at[j], peer)

    def send_acts(d):
        @pl.when(z + d <= n - 1)
        def _():
            send_block(z + d).start()

        @pl.when(jnp.logical_and(d > 0, z - d >= 0))
        def _():
            send_block(z - d).start()

    def z_copy(buf, slot_at, way, t_send, t_recv, c, target):
        at = buf.at[slot_at, chunk_rows(c)]
        return remote(at, at, z_tx.at[way, t_send, c], z_rx.at[way, t_recv, c], target)

    def w_send(way, j, t, target):
        @pl.loop(0, CHUNKS)
        def _(c):
            z_copy(w_all, j, way, t, t, c, target).start()

    def w_relay(way, j, t, target, further):
        @pl.loop(0, CHUNKS)
        def _(c):
            z_copy(w_all, j, way, t, t - 1, c, peer).wait_recv()

            @pl.when(further)
            def _():
                z_copy(w_all, j, way, t, t, c, target).start()

    def load_state(c):
        at = lax.rem(c, 2)
        return [
            pltpu.make_async_copy(array.at[chunk_rows(c)], state.at[at, i], state_sem.at[at, i])
            for i, array in enumerate((inner_w, adam_m, adam_v, anchor))
        ]

    own_w = pltpu.make_async_copy(w_own, w_all.at[z], local_sem.at[0])
    own_g = pltpu.make_async_copy(grads, cot.at[pl.ds(0, rows)], local_sem.at[1])
    own_w.start()
    own_g.start()
    for c in range(2):
        for copy in load_state(c):
            copy.start()

    @pl.loop(0, n)
    def _(j):
        load_acts(j).start()

    all_sums[me] = sums[...]

    barrier = pltpu.get_barrier_semaphore()

    @pl.loop(1, size)
    def _(k):
        pl.semaphore_signal(
            barrier, inc=1, device_id={"fsdp": lax.rem(me + k, size)}, device_id_type=MESH)

    pl.semaphore_signal(barrier, inc=1, device_id={"rep": core_peer}, device_id_type=MESH)
    for k in range(1, pairs_y):
        pl.semaphore_signal(barrier, inc=1, device_id={"rep": y_peer(k)}, device_id_type=MESH)
    pl.semaphore_wait(barrier, size - 1 + pairs_y)

    @pl.loop(1, size)
    def _(k):
        remote(sums, all_sums.at[me], sums_tx.at[k], sums_rx.at[me], lax.rem(me + k, size)).start()

    peer_g = remote(grads, cot.at[pl.ds(rows, rows)], g_sem.at[0], g_sem.at[1], peer)
    peer_g.start()
    own_w.wait()

    @pl.when(z < n - 1)
    def _():
        w_send(0, z, 0, above)

    @pl.when(z > 0)
    def _():
        w_send(1, z, 0, below)

    send_acts(n - 1)

    @pl.loop(1, size)
    def _(k):
        source = lax.rem(me + k, size)
        remote(sums, all_sums.at[source], sums_tx.at[k], sums_rx.at[source], peer).wait_recv()

    own_g.wait()
    peer_g.wait_recv()
    if n >= 2:
        send_acts(n - 2)
    half_n = size * seqs // 2
    for q in range(2 * seqs):
        owner = me if q < seqs else peer
        seq = owner * seqs + q % seqs
        margin = dpo_beta * jnp.sum(jnp.sum(all_sums[...] * signs[q], axis=0), axis=0, keepdims=True)
        pull = 1.0 / (1.0 + jnp.exp(margin))
        weight = jnp.where(seq < half_n, -dpo_beta, dpo_beta) * pull
        span = pl.ds(q * SEQLEN, SEQLEN)
        for lane in range(0, width, 128):
            cell = cot[span, lane:lane + 128].astype(jnp.float32)
            cot[span, lane:lane + 128] = (weight * cell).astype(jnp.bfloat16)

    def partial(j):
        load_acts(j).wait()
        send_block(j).wait_recv()

        @pl.loop(0, parts)
        def _(c):
            span = pl.ds(pl.multiple_of(c * part, part), part)
            grad[span, :] = scale * lax.dot_general(
                act[j, :, span], cot[...], (((0,), (0,)), ((), ())), preferred_element_type=jnp.float32)

    def pass_on(way, j, t):
        at = j + 1 if way == 0 else j
        has_source = z > 0 if way == 0 else z < n - 1
        target = above if way == 0 else below
        partial(j)

        @pl.loop(0, CHUNKS)
        def _(c):
            span = chunk_rows(c)

            @pl.when(has_source)
            def _():
                z_copy(running, at, way, t, t - 1, c, peer).wait_recv()
                running[at, span, :] = (
                    grad[span, :] + running[at, span, :].astype(jnp.float32)).astype(jnp.bfloat16)

            @pl.when(jnp.logical_not(has_source))
            def _():
                running[at, span, :] = grad[span, :].astype(jnp.bfloat16)

            z_copy(running, at, way, t, t, c, target).start()

    def ig_keep(j):
        return pltpu.make_async_copy(
            stage.at[j, pl.ds(0, rows)], input_grad.at[:, columns(j * 2 + x)], ig_local.at[j])

    def ig_send(j):
        return remote(
            stage.at[j, pl.ds(rows, rows)], input_grad.at[:, columns(j * 2 + x)], ig_tx.at[j], ig_rx.at[j], peer)

    def ig_arrival(j):
        return remote(
            stage.at[j, pl.ds(rows, rows)], input_grad.at[:, columns(j * 2 + 1 - x)], ig_tx.at[j], ig_rx.at[j], peer)

    def ig_block(j):
        @pl.loop(0, parts)
        def _(c):
            span = pl.ds(pl.multiple_of(c * part, part), part)
            stage[j, :, span] = (scale * lax.dot_general(
                cot[...], w_all[j, span, :], (((1,), (1,)), ((), ())), preferred_element_type=jnp.float32
            )).astype(jnp.bfloat16)

        ig_keep(j).start()
        ig_send(j).start()

    def slot(t, carry):
        d = n - t

        @pl.when(z >= t)
        def _():
            w_relay(0, z - t, t, above, z < n - 1)

        @pl.when(z + t <= n - 1)
        def _():
            w_relay(1, z + t, t, below, z > 0)

        @pl.when(z + d <= n - 1)
        def _():
            pass_on(0, z + d, t)

        @pl.when(z - d >= 0)
        def _():
            pass_on(1, z - d, t)

        @pl.when(d >= 2)
        def _():
            send_acts(d - 2)

        @pl.when(t == 1)
        def _():
            ig_block(z)

        @pl.when(z >= t)
        def _():
            ig_block(z - t)

        @pl.when(z + t <= n - 1)
        def _():
            ig_block(z + t)

        return carry

    lax.fori_loop(1, n, slot, 0)

    def core_send(c):
        return remote(
            delta.at[half_rows(c, 1 - core)], core_in.at[packed_rows(c)],
            core_tx.at[c], core_rx.at[c], core_peer, "rep")

    def y_send(c, k):
        at = y_parts.at[y, packed_rows(c)]
        return remote(at, at, y_tx.at[k, c], y_rx.at[y, c], y_peer(k), "rep")

    def y_arrival(c, k):
        source = lax.rem(y + k, pairs_y)
        at = y_parts.at[source, packed_rows(c)]
        return remote(at, at, y_tx.at[k, c], y_rx.at[source, c], y_peer(k), "rep")

    def back_send(c, which):
        at = delta_sum.at[half_rows(c, which)]
        return remote(at, at, back_tx.at[c], back_rx.at[c], core_peer, "rep")

    def inner_step(c):
        span = chunk_rows(c)

        @pl.when(z > 0)
        def _():
            z_copy(running, z + 1, 0, n - 1, n - 1, c, peer).wait_recv()
            grad[span, :] = grad[span, :] + running[z + 1, span, :].astype(jnp.float32)

        @pl.when(z < n - 1)
        def _():
            z_copy(running, z, 1, n - 1, n - 1, c, peer).wait_recv()
            grad[span, :] = grad[span, :] + running[z, span, :].astype(jnp.float32)

        for copy in load_state(c):
            copy.wait()
        at = lax.rem(c, 2)
        g = grad[span, :]
        weights = state[at, 0]
        m_next = decay_one * state[at, 1] + (1.0 - decay_one) * g
        v_next = decay_two * state[at, 2] + (1.0 - decay_two) * g * g
        inner_next = weights - inner_rate * (m_next / (jnp.sqrt(v_next) + epsilon) + weight_decay * weights)
        delta[span, :] = state[at, 3] - inner_next
        core_send(c).start()

        @pl.when(c + 2 < CHUNKS)
        def _():
            for copy in load_state(c + 2):
                copy.start()

    def over_y(c):
        core_send(c).wait_recv()
        y_parts[y, packed_rows(c), :] = (
            delta[half_rows(c, core), :] + core_in[packed_rows(c), :]).astype(jnp.bfloat16)
        for k in range(1, pairs_y):
            y_send(c, k).start()

    def back(c):
        for k in range(1, pairs_y):
            y_arrival(c, k).wait_recv()
        total = y_parts[0, packed_rows(c), :].astype(jnp.float32)
        for i in range(1, pairs_y):
            total = total + y_parts[i, packed_rows(c), :].astype(jnp.float32)
        delta_sum[half_rows(c, core), :] = total
        back_send(c, core).start()

    partial(z)

    @pl.loop(0, CHUNKS)
    def _(c):
        inner_step(c)
        over_y(c)

        @pl.when(c > 0)
        def _():
            back(c - 1)

    back(CHUNKS - 1)

    @pl.loop(0, CHUNKS)
    def _(c):
        back_send(c, 1 - core).wait_recv()
        back_send(c, core).wait_send()
        core_send(c).wait_send()
        for k in range(1, pairs_y):
            y_send(c, k).wait_send()

    @pl.loop(1, size)
    def _(k):
        remote(sums, all_sums.at[me], sums_tx.at[k], sums_rx.at[me], peer).wait_send()

    peer_g.wait_send()

    @pl.loop(0, n)
    def _(j):
        send_block(j).wait_send()

        @pl.loop(0, CHUNKS)
        def _(c):
            @pl.when(z < n - 1)
            def _():
                z_copy(w_all, j, 0, j, j, c, peer).wait_send()

            @pl.when(z > 0)
            def _():
                z_copy(w_all, j, 1, j, j, c, peer).wait_send()

        ig_keep(j).wait()
        ig_send(j).wait_send()
        ig_arrival(j).wait_recv()


def exchange(size, groups, scale, acts, grads, w_half, sums, signs, inner_w, adam_m, adam_v, anchor):
    n = size // 2
    rows, model = acts.shape
    feats, width = w_half.shape
    dma = pltpu.SemaphoreType.DMA
    bf16 = jnp.bfloat16
    anywhere = pl.BlockSpec(memory_space=pl.ANY)
    vmem = pl.BlockSpec(memory_space=pltpu.VMEM)
    return pl.pallas_call(
        functools.partial(exchange_kernel, size, groups, scale),
        out_shape=(
            jax.ShapeDtypeStruct((rows, model), bf16),
            jax.ShapeDtypeStruct((feats, width), jnp.float32),
            jax.ShapeDtypeStruct((feats, width), jnp.float32),
        ),
        in_specs=[anywhere, anywhere, anywhere, vmem, vmem] + [anywhere] * 4,
        out_specs=(anywhere, vmem, vmem),
        scratch_shapes=[
            pltpu.VMEM((size,) + sums.shape, jnp.float32),
            pltpu.VMEM((n, 2 * rows, feats), bf16),
            pltpu.VMEM((2 * rows, width), bf16),
            pltpu.VMEM((n, feats, width), bf16),
            pltpu.VMEM((n + 1, feats, width), bf16),
            pltpu.VMEM((n, 2 * rows, feats), bf16),
            pltpu.VMEM((2, 4, feats // CHUNKS, width), jnp.float32),
            pltpu.VMEM((feats, width), jnp.float32),
            pltpu.VMEM((feats // 2, width), jnp.float32),
            pltpu.VMEM((groups // 2, feats // 2, width), bf16),
            dma((size,)), dma((size,)), dma((2,)), dma((2,)),
            dma((n,)), dma((n,)), dma((n,)),
            dma((2, n, CHUNKS)), dma((2, n, CHUNKS)),
            dma((n,)), dma((n,)), dma((n,)),
            dma((2, 4)), dma((CHUNKS,)), dma((CHUNKS,)),
            dma((groups // 2, CHUNKS)), dma((groups // 2, CHUNKS)), dma((CHUNKS,)), dma((CHUNKS,)),
        ],
        compiler_params=pltpu.CompilerParams(
            collective_id=0, has_side_effects=True, vmem_limit_bytes=62 * 1024 * 1024),
        cost_estimate=pl.CostEstimate(
            flops=8 * rows * model * width, bytes_accessed=6 * rows * model, transcendentals=0),
    )(acts, grads, w_half, sums, signs, inner_w, adam_m, adam_v, anchor)


def outer_step(delta_avg, anchor_rows, mom_rows):
    mom_next = momentum * mom_rows + delta_avg
    anchor_next = anchor_rows - outer_rate * (delta_avg + momentum * mom_next)
    return (anchor_next, mom_next)


def local(acts, tok_grads, log_ratio, loss_mask, pairs, inner_w, adam_m, adam_v, anchor, outer_mom):
    size = lax.axis_size("fsdp")
    rows, model = acts.shape
    seqs = rows // SEQLEN
    scale = model ** (-0.5)
    mask_f = loss_mask.astype(jnp.float32)
    own_sums = (log_ratio * mask_f).reshape(seqs, SEQLEN).sum(axis=1)
    tile = -(-seqs // 8) * 8
    sums = jnp.zeros((tile, 128), jnp.float32).at[:seqs].set(jnp.broadcast_to(own_sums[:, None], (seqs, 128)))
    me = lax.axis_index("fsdp")
    peer = me + 1 - 2 * lax.rem(me, 2)
    table = pair_signs(pairs[0], size * seqs // 2)
    ours = jnp.concatenate([
        lax.dynamic_slice_in_dim(table, me * seqs, seqs),
        lax.dynamic_slice_in_dim(table, peer * seqs, seqs),
    ]).reshape(2 * seqs, size, seqs)
    signs = jnp.broadcast_to(
        jnp.pad(ours, ((0, 0), (0, 0), (0, tile - seqs)))[..., None], (2 * seqs, size, tile, 128))
    grads = jnp.where(loss_mask[:, None] != 0, tok_grads, jnp.zeros_like(tok_grads))
    w_half = inner_w[0].astype(jnp.bfloat16)
    groups = lax.axis_size("rep")
    input_grad, grad, delta_sum = exchange(
        size, groups, scale, acts, grads, w_half, sums, signs, inner_w[0], adam_m[0], adam_v[0], anchor)
    m_next = decay_one * adam_m[0] + (1.0 - decay_one) * grad
    delta_avg = delta_sum / groups
    new_anchor, new_mom = outer_step(delta_avg, anchor, outer_mom)
    return (input_grad, new_anchor, new_mom, m_next[None])


def solution(mesh):
    return jax.shard_map(
        local,
        mesh=mesh,
        in_specs=(
            P(("rep", "fsdp"), None),
            P(("rep", "fsdp"), None),
            P(("rep", "fsdp")),
            P(("rep", "fsdp")),
            P("rep", None),
            P("rep", "fsdp", None),
            P("rep", "fsdp", None),
            P("rep", "fsdp", None),
            P("fsdp", None),
            P("fsdp", None),
        ),
        out_specs=(
            P(("rep", "fsdp"), None),
            P("fsdp", None),
            P("fsdp", None),
            P("rep", "fsdp", None),
        ),
        check_vma=False,
    )
```

```python
import functools

import jax
import jax.numpy as jnp
from jax import lax
from jax.experimental import pallas as pl
from jax.experimental.pallas import tpu as pltpu
from jax.sharding import PartitionSpec as P

SEQLEN = 256

dpo_beta = 0.1
decay_one = 0.9
decay_two = 0.95
inner_rate = 0.05
weight_decay = 0.1
epsilon = 1e-08
momentum = 0.9
outer_rate = 0.7

CHUNKS = 8

MESH = pl.DeviceIdType.MESH


def pair_signs(partner, half_n):
    cols = jnp.arange(2 * half_n, dtype=jnp.int32)[None, :]
    chosen = jnp.arange(half_n, dtype=jnp.int32)[:, None]
    of_pair = (cols == chosen).astype(jnp.float32) - (cols == half_n + partner[:, None]).astype(jnp.float32)
    onehot = (partner[:, None] == jnp.arange(half_n, dtype=jnp.int32)[None, :]).astype(jnp.float32)
    of_rejected = jnp.sum(onehot[:, :, None] * of_pair[:, None, :], axis=0)
    return jnp.concatenate([of_pair, of_rejected])


def exchange_kernel(
    size, groups, scale, acts, grads, sums, signs, inner_w, adam_m, adam_v, anchor,
    input_grad, grad, delta_sum,
    all_sums, act, cot, w_all, running, stage, state, delta, core_in, y_parts,
    sums_tx, sums_rx, g_sem, local_sem, act_local, act_tx, act_rx, z_tx, z_rx, ig_local, ig_tx, ig_rx,
    state_sem, core_tx, core_rx, y_tx, y_rx, back_tx, back_rx,
):
    n = size // 2
    me = lax.axis_index("fsdp")
    z, x = lax.div(me, 2), lax.rem(me, 2)
    peer = z * 2 + (1 - x)
    above, below = lax.rem(me + 2, size), lax.rem(me + size - 2, size)
    rows = acts.shape[0]
    feats, width = inner_w.shape
    part = min(256, feats)
    parts = feats // part
    seqs = rows // SEQLEN
    chunk = feats // CHUNKS
    half = chunk // 2
    pairs_y = groups // 2
    group = lax.axis_index("rep")
    y, core = lax.div(group, 2), lax.rem(group, 2)
    core_peer = y * 2 + (1 - core)

    def remote(src, dst, tx, rx, target, axis="fsdp"):
        return pltpu.make_async_remote_copy(
            src_ref=src, dst_ref=dst, send_sem=tx, recv_sem=rx,
            device_id={axis: target}, device_id_type=MESH,
        )

    def y_peer(k):
        return lax.rem(y + k, pairs_y) * 2 + core

    def chunk_rows(c):
        return pl.ds(pl.multiple_of(c * chunk, chunk), chunk)

    def half_rows(c, which):
        return pl.ds(pl.multiple_of(c * chunk + which * half, half), half)

    def packed_rows(c):
        return pl.ds(pl.multiple_of(c * half, half), half)

    def columns(block):
        return pl.ds(pl.multiple_of(block * feats, feats), feats)

    def load_acts(j):
        return pltpu.make_async_copy(
            acts.at[:, columns(j * 2 + x)], act.at[j, pl.ds(0, rows)], act_local.at[j])

    def send_block(j):
        return remote(
            acts.at[:, columns(j * 2 + 1 - x)], act.at[j, pl.ds(rows, rows)], act_tx.at[j], act_rx.at[j], peer)

    def send_acts(d):
        @pl.when(z + d <= n - 1)
        def _():
            send_block(z + d).start()

        @pl.when(jnp.logical_and(d > 0, z - d >= 0))
        def _():
            send_block(z - d).start()

    def z_copy(buf, slot_at, way, t_send, t_recv, c, target):
        at = buf.at[slot_at, chunk_rows(c)]
        return remote(at, at, z_tx.at[way, t_send, c], z_rx.at[way, t_recv, c], target)

    def w_send(way, j, t, target):
        @pl.loop(0, CHUNKS)
        def _(c):
            z_copy(w_all, j, way, t, t, c, target).start()

    def w_relay(way, j, t, target):
        @pl.loop(0, CHUNKS)
        def _(c):
            z_copy(w_all, j, way, t, t - 1, c, peer).wait_recv()
            z_copy(w_all, j, way, t, t, c, target).start()

    def w_arrive(way, j, t):
        @pl.loop(0, CHUNKS)
        def _(c):
            z_copy(w_all, j, way, t, t - 1, c, peer).wait_recv()

    def load_state(c):
        at = lax.rem(c, 2)
        return [
            pltpu.make_async_copy(array.at[chunk_rows(c)], state.at[at, i], state_sem.at[at, i])
            for i, array in enumerate((inner_w, adam_m, adam_v, anchor))
        ]

    own_w = pltpu.make_async_copy(inner_w, grad, local_sem.at[0])
    own_g = pltpu.make_async_copy(grads, cot.at[pl.ds(0, rows)], local_sem.at[1])
    own_w.start()
    own_g.start()
    for c in range(2):
        for copy in load_state(c):
            copy.start()

    @pl.loop(0, n)
    def _(j):
        load_acts(j).start()

    all_sums[me] = sums[...]

    barrier = pltpu.get_barrier_semaphore()

    @pl.loop(1, size)
    def _(k):
        pl.semaphore_signal(
            barrier, inc=1, device_id={"fsdp": lax.rem(me + k, size)}, device_id_type=MESH)

    pl.semaphore_signal(barrier, inc=1, device_id={"rep": core_peer}, device_id_type=MESH)
    for k in range(1, pairs_y):
        pl.semaphore_signal(barrier, inc=1, device_id={"rep": y_peer(k)}, device_id_type=MESH)

    own_w.wait()

    @pl.loop(0, CHUNKS)
    def _(c):
        w_all[z, chunk_rows(c), :] = grad[chunk_rows(c), :].astype(jnp.bfloat16)

    pl.semaphore_wait(barrier, size - 1 + pairs_y)

    @pl.loop(1, size)
    def _(k):
        remote(sums, all_sums.at[me], sums_tx.at[k], sums_rx.at[me], lax.rem(me + k, size)).start()

    peer_g = remote(grads, cot.at[pl.ds(rows, rows)], g_sem.at[0], g_sem.at[1], peer)
    peer_g.start()

    @pl.when(z < n - 1)
    def _():
        w_send(0, z, 0, above)

    @pl.when(z > 0)
    def _():
        w_send(1, z, 0, below)

    farthest = jnp.maximum(z, n - 1 - z)
    send_acts(farthest)

    @pl.loop(1, size)
    def _(k):
        source = lax.rem(me + k, size)
        remote(sums, all_sums.at[source], sums_tx.at[k], sums_rx.at[source], peer).wait_recv()

    own_g.wait()
    peer_g.wait_recv()
    send_acts(farthest - 1)
    half_n = size * seqs // 2
    for q in range(2 * seqs):
        owner = me if q < seqs else peer
        seq = owner * seqs + q % seqs
        margin = dpo_beta * jnp.sum(jnp.sum(all_sums[...] * signs[q], axis=0), axis=0, keepdims=True)
        pull = 1.0 / (1.0 + jnp.exp(margin))
        weight = jnp.where(seq < half_n, -dpo_beta, dpo_beta) * pull
        span = pl.ds(q * SEQLEN, SEQLEN)
        for lane in range(0, width, 128):
            cell = cot[span, lane:lane + 128].astype(jnp.float32)
            cot[span, lane:lane + 128] = (weight * cell).astype(jnp.bfloat16)

    def partial(j):
        load_acts(j).wait()
        send_block(j).wait_recv()

        @pl.loop(0, parts)
        def _(c):
            span = pl.ds(pl.multiple_of(c * part, part), part)
            grad[span, :] = scale * lax.dot_general(
                act[j, :, span], cot[...], (((0,), (0,)), ((), ())), preferred_element_type=jnp.float32)

    def pass_on(way, j, t):
        at = j + 1 if way == 0 else j
        has_source = z > 0 if way == 0 else z < n - 1
        target = above if way == 0 else below

        @pl.loop(0, CHUNKS)
        def _(c):
            span = chunk_rows(c)

            @pl.when(has_source)
            def _():
                z_copy(running, at, way, t, t - 1, c, peer).wait_recv()
                running[at, span, :] = (
                    grad[span, :] + running[at, span, :].astype(jnp.float32)).astype(jnp.bfloat16)

            @pl.when(jnp.logical_not(has_source))
            def _():
                running[at, span, :] = grad[span, :].astype(jnp.bfloat16)

            z_copy(running, at, way, t, t, c, target).start()

    def ig_keep(j):
        return pltpu.make_async_copy(
            stage.at[j, pl.ds(0, rows)], input_grad.at[:, columns(j * 2 + x)], ig_local.at[j])

    def ig_send(j):
        return remote(
            stage.at[j, pl.ds(rows, rows)], input_grad.at[:, columns(j * 2 + x)], ig_tx.at[j], ig_rx.at[j], peer)

    def ig_arrival(j):
        return remote(
            stage.at[j, pl.ds(rows, rows)], input_grad.at[:, columns(j * 2 + 1 - x)], ig_tx.at[j], ig_rx.at[j], peer)

    def ig_block(j):
        @pl.loop(0, parts)
        def _(c):
            span = pl.ds(pl.multiple_of(c * part, part), part)
            stage[j, :, span] = (scale * lax.dot_general(
                cot[...], w_all[j, span, :], (((1,), (1,)), ((), ())), preferred_element_type=jnp.float32
            )).astype(jnp.bfloat16)

        ig_keep(j).start()
        ig_send(j).start()

    def slot(t, carry):
        d = n - t

        sum_up = z + d <= n - 1
        sum_down = z - d >= 0
        both = jnp.logical_and(sum_up, sum_down)

        @pl.when(sum_up)
        def _():
            partial(z + d)

        @pl.when(jnp.logical_and(sum_down, jnp.logical_not(sum_up)))
        def _():
            partial(z - d)

        @pl.when(jnp.logical_and(z >= t, z < n - 1))
        def _():
            w_relay(0, z - t, t, above)

        @pl.when(jnp.logical_and(z + t <= n - 1, z > 0))
        def _():
            w_relay(1, z + t, t, below)

        @pl.when(sum_up)
        def _():
            pass_on(0, z + d, t)

        @pl.when(both)
        def _():
            partial(z - d)

        @pl.when(sum_down)
        def _():
            pass_on(1, z - d, t)

        @pl.when(farthest - 1 - t >= 0)
        def _():
            send_acts(farthest - 1 - t)

        @pl.when(t == 1)
        def _():
            ig_block(z)

        @pl.when(z >= t)
        def _():
            @pl.when(z == n - 1)
            def _():
                w_arrive(0, z - t, t)

            ig_block(z - t)

        @pl.when(z + t <= n - 1)
        def _():
            @pl.when(z == 0)
            def _():
                w_arrive(1, z + t, t)

            ig_block(z + t)

        return carry

    lax.fori_loop(1, n, slot, 0)

    def core_send(c):
        return remote(
            delta.at[half_rows(c, 1 - core)], core_in.at[packed_rows(c)],
            core_tx.at[c], core_rx.at[c], core_peer, "rep")

    def y_send(c, k):
        at = y_parts.at[y, packed_rows(c)]
        return remote(at, at, y_tx.at[k, c], y_rx.at[y, c], y_peer(k), "rep")

    def y_arrival(c, k):
        source = lax.rem(y + k, pairs_y)
        at = y_parts.at[source, packed_rows(c)]
        return remote(at, at, y_tx.at[k, c], y_rx.at[source, c], y_peer(k), "rep")

    def back_send(c, which):
        at = delta_sum.at[half_rows(c, which)]
        return remote(at, at, back_tx.at[c], back_rx.at[c], core_peer, "rep")

    def inner_step(c):
        span = chunk_rows(c)

        @pl.when(z > 0)
        def _():
            z_copy(running, z + 1, 0, n - 1, n - 1, c, peer).wait_recv()
            grad[span, :] = grad[span, :] + running[z + 1, span, :].astype(jnp.float32)

        @pl.when(z < n - 1)
        def _():
            z_copy(running, z, 1, n - 1, n - 1, c, peer).wait_recv()
            grad[span, :] = grad[span, :] + running[z, span, :].astype(jnp.float32)

        for copy in load_state(c):
            copy.wait()
        at = lax.rem(c, 2)
        g = grad[span, :]
        weights = state[at, 0]
        m_next = decay_one * state[at, 1] + (1.0 - decay_one) * g
        v_next = decay_two * state[at, 2] + (1.0 - decay_two) * g * g
        inner_next = weights - inner_rate * (m_next / (jnp.sqrt(v_next) + epsilon) + weight_decay * weights)
        delta[span, :] = state[at, 3] - inner_next
        core_send(c).start()

        @pl.when(c + 2 < CHUNKS)
        def _():
            for copy in load_state(c + 2):
                copy.start()

    def over_y(c):
        core_send(c).wait_recv()
        y_parts[y, packed_rows(c), :] = (
            delta[half_rows(c, core), :] + core_in[packed_rows(c), :]).astype(jnp.bfloat16)
        for k in range(1, pairs_y):
            y_send(c, k).start()

    def back(c):
        for k in range(1, pairs_y):
            y_arrival(c, k).wait_recv()
        total = y_parts[0, packed_rows(c), :].astype(jnp.float32)
        for i in range(1, pairs_y):
            total = total + y_parts[i, packed_rows(c), :].astype(jnp.float32)
        delta_sum[half_rows(c, core), :] = total
        back_send(c, core).start()

    partial(z)

    @pl.loop(0, CHUNKS)
    def _(c):
        inner_step(c)
        over_y(c)

        @pl.when(c > 0)
        def _():
            back(c - 1)

    back(CHUNKS - 1)

    @pl.loop(0, CHUNKS)
    def _(c):
        back_send(c, 1 - core).wait_recv()
        back_send(c, core).wait_send()
        core_send(c).wait_send()
        for k in range(1, pairs_y):
            y_send(c, k).wait_send()

    @pl.loop(1, size)
    def _(k):
        remote(sums, all_sums.at[me], sums_tx.at[k], sums_rx.at[me], peer).wait_send()

    peer_g.wait_send()

    @pl.loop(0, n)
    def _(j):
        send_block(j).wait_send()

        @pl.loop(0, CHUNKS)
        def _(c):
            @pl.when(z < n - 1)
            def _():
                z_copy(w_all, j, 0, j, j, c, peer).wait_send()

            @pl.when(z > 0)
            def _():
                z_copy(w_all, j, 1, j, j, c, peer).wait_send()

        ig_keep(j).wait()
        ig_send(j).wait_send()
        ig_arrival(j).wait_recv()


def exchange(size, groups, scale, acts, grads, sums, signs, inner_w, adam_m, adam_v, anchor):
    n = size // 2
    rows, model = acts.shape
    feats, width = inner_w.shape
    dma = pltpu.SemaphoreType.DMA
    bf16 = jnp.bfloat16
    anywhere = pl.BlockSpec(memory_space=pl.ANY)
    vmem = pl.BlockSpec(memory_space=pltpu.VMEM)
    return pl.pallas_call(
        functools.partial(exchange_kernel, size, groups, scale),
        out_shape=(
            jax.ShapeDtypeStruct((rows, model), bf16),
            jax.ShapeDtypeStruct((feats, width), jnp.float32),
            jax.ShapeDtypeStruct((feats, width), jnp.float32),
        ),
        in_specs=[anywhere, anywhere, vmem, vmem] + [anywhere] * 4,
        out_specs=(anywhere, vmem, vmem),
        scratch_shapes=[
            pltpu.VMEM((size,) + sums.shape, jnp.float32),
            pltpu.VMEM((n, 2 * rows, feats), bf16),
            pltpu.VMEM((2 * rows, width), bf16),
            pltpu.VMEM((n, feats, width), bf16),
            pltpu.VMEM((n + 1, feats, width), bf16),
            pltpu.VMEM((n, 2 * rows, feats), bf16),
            pltpu.VMEM((2, 4, feats // CHUNKS, width), jnp.float32),
            pltpu.VMEM((feats, width), jnp.float32),
            pltpu.VMEM((feats // 2, width), jnp.float32),
            pltpu.VMEM((groups // 2, feats // 2, width), bf16),
            dma((size,)), dma((size,)), dma((2,)), dma((2,)),
            dma((n,)), dma((n,)), dma((n,)),
            dma((2, n, CHUNKS)), dma((2, n, CHUNKS)),
            dma((n,)), dma((n,)), dma((n,)),
            dma((2, 4)), dma((CHUNKS,)), dma((CHUNKS,)),
            dma((groups // 2, CHUNKS)), dma((groups // 2, CHUNKS)), dma((CHUNKS,)), dma((CHUNKS,)),
        ],
        compiler_params=pltpu.CompilerParams(
            collective_id=0, has_side_effects=True, vmem_limit_bytes=62 * 1024 * 1024),
        cost_estimate=pl.CostEstimate(
            flops=8 * rows * model * width, bytes_accessed=6 * rows * model, transcendentals=0),
    )(acts, grads, sums, signs, inner_w, adam_m, adam_v, anchor)


def outer_step(delta_avg, anchor_rows, mom_rows):
    mom_next = momentum * mom_rows + delta_avg
    anchor_next = anchor_rows - outer_rate * (delta_avg + momentum * mom_next)
    return (anchor_next, mom_next)


def local(acts, tok_grads, log_ratio, loss_mask, pairs, inner_w, adam_m, adam_v, anchor, outer_mom):
    size = lax.axis_size("fsdp")
    rows, model = acts.shape
    seqs = rows // SEQLEN
    scale = model ** (-0.5)
    mask_f = loss_mask.astype(jnp.float32)
    own_sums = (log_ratio * mask_f).reshape(seqs, SEQLEN).sum(axis=1)
    tile = -(-seqs // 8) * 8
    sums = jnp.zeros((tile, 128), jnp.float32).at[:seqs].set(jnp.broadcast_to(own_sums[:, None], (seqs, 128)))
    me = lax.axis_index("fsdp")
    peer = me + 1 - 2 * lax.rem(me, 2)
    table = pair_signs(pairs[0], size * seqs // 2)
    ours = jnp.concatenate([
        lax.dynamic_slice_in_dim(table, me * seqs, seqs),
        lax.dynamic_slice_in_dim(table, peer * seqs, seqs),
    ]).reshape(2 * seqs, size, seqs)
    signs = jnp.broadcast_to(
        jnp.pad(ours, ((0, 0), (0, 0), (0, tile - seqs)))[..., None], (2 * seqs, size, tile, 128))
    grads = jnp.where(loss_mask[:, None] != 0, tok_grads, jnp.zeros_like(tok_grads))
    groups = lax.axis_size("rep")
    input_grad, grad, delta_sum = exchange(
        size, groups, scale, acts, grads, sums, signs, inner_w[0], adam_m[0], adam_v[0], anchor)
    m_next = decay_one * adam_m[0] + (1.0 - decay_one) * grad
    delta_avg = delta_sum / groups
    new_anchor, new_mom = outer_step(delta_avg, anchor, outer_mom)
    return (input_grad, new_anchor, new_mom, m_next[None])


def solution(mesh):
    return jax.shard_map(
        local,
        mesh=mesh,
        in_specs=(
            P(("rep", "fsdp"), None),
            P(("rep", "fsdp"), None),
            P(("rep", "fsdp")),
            P(("rep", "fsdp")),
            P("rep", None),
            P("rep", "fsdp", None),
            P("rep", "fsdp", None),
            P("rep", "fsdp", None),
            P("fsdp", None),
            P("fsdp", None),
        ),
        out_specs=(
            P(("rep", "fsdp"), None),
            P("fsdp", None),
            P("fsdp", None),
            P("rep", "fsdp", None),
        ),
        check_vma=False,
    )
```
